32 devices in a mesh: dev: 32 (over z, y, x, core).
Axes of the slice: x: 2, y: 2, z: 4, core: 2. Of those that a mesh axis runs over, the one named last changes fastest.
Arguments:
- source_rows: bfloat16 [32768, 4096], P('dev'), may hold values from -6 to 6
- factor: bfloat16 [8, 512, 512], replicated, may hold values from -0.25 to 0.25
- plan_start: int32 [32, 32], replicated, may hold values from 0 to 992, as said below
- plan_count: int32 [32, 32], replicated, may hold values from 0 to 32, as said below
- partners: int32 [2, 32], replicated, may hold values from 0 to 31, as said below
Outputs:
- kernel_tiles: float32 [2, 16384, 512], P(None, 'dev')
The draws below stay inside these ranges and needn't reach their ends.
Inputs may be any that keep to these rules, and one draw needn't show every extreme that they name: `plan_count`: entry [s, d] is how many rows source shard s sends to destination d; each column sums to exactly 512; one source's counts sum to at most 1024, and some source reaches it. `plan_start`: the row ranges of one source for the different destinations are disjoint and lie within its 1024 rows. In each round r there is one power of two m_r with partners[r, d] = d XOR m_r for every player d; the m_r of different rounds differ.
All inputs are finite; a program needn't handle non-finite values.
Results may differ from the reference program's by a relative error of at most 0.0029.
Values may be sent and summed in bfloat16 or wider, within the bound.
A program may use at most 128 MiB of HBM per device.

```python
import jax
import jax.numpy as jnp
from jax import lax

BLOCK = 512
LAYERS = 8
ROWS_DEV = 512
ROUNDS = 2
FEATS = 4096
SRC_CAP = 1024
ROWS = 16384
N_DEV = 32


def plan_tables(key):
    base_key = jax.random.fold_in(key, 4242)
    key_bias, key_mix, key_force, key_split, key_order = jax.random.split(base_key, 5)
    half_count = N_DEV // 2
    slot_rows = 2 * ROWS_DEV // N_DEV
    source_bias = jax.random.randint(key_bias, (N_DEV,), 0, 4)
    forced = jax.random.randint(key_force, (), 0, N_DEV)
    source_bias = jnp.where(jnp.arange(N_DEV) == forced, 10, source_bias)
    mixing = jax.random.randint(key_mix, (N_DEV, N_DEV), 0, 2 * N_DEV)
    scores = (source_bias[:, None] * N_DEV + mixing) * N_DEV + jnp.arange(N_DEV)[:, None]
    order_rank = jnp.argsort(-scores, axis=0)
    rank_in_column = jnp.argsort(order_rank, axis=0)
    split_share = jax.random.randint(key_split, (N_DEV,), 1, slot_rows)
    counts_table = jnp.where(rank_in_column < half_count - 1, slot_rows, 0)
    counts_table = jnp.where(rank_in_column == half_count - 1, split_share[None, :], counts_table)
    counts_table = jnp.where(rank_in_column == half_count, slot_rows - split_share[None, :], counts_table)
    order_keys = jax.random.randint(key_order, (N_DEV, N_DEV), 0, 1 << 20) * N_DEV + jnp.arange(N_DEV)[None, :]
    order_dest = jnp.argsort(order_keys, axis=1)
    ordered = jnp.take_along_axis(counts_table, order_dest, axis=1)
    prefix = jnp.cumsum(ordered, axis=1) - ordered
    starts_table = jnp.take_along_axis(prefix, jnp.argsort(order_dest, axis=1), axis=1)
    return (starts_table.astype(jnp.int32), counts_table.astype(jnp.int32))


def draw_plan_start(key, part):
    return plan_tables(key)[0]


def draw_plan_count(key, part):
    return plan_tables(key)[1]


def draw_partners(key, part):
    base_key = jax.random.fold_in(key, 777)
    levels = N_DEV.bit_length() - 1
    chosen = jax.random.permutation(base_key, levels).astype(jnp.int32)
    positions = jnp.arange(N_DEV, dtype=jnp.int32)
    tables = []
    for round_index in range(ROUNDS):
        mask_value = jnp.left_shift(jnp.int32(1), chosen[round_index]).astype(jnp.int32)
        tables.append(jnp.bitwise_xor(positions, mask_value).astype(jnp.int32))
    return jnp.stack(tables).astype(jnp.int32)


def block_levels(own_key, shape, shards, least, top_value):
    factor_of = 1.0
    for axis_at, parts in shards:
        draws = jax.random.uniform(jax.random.fold_in(jax.random.fold_in(own_key, 6), axis_at), (parts,), jnp.float32, least / len(shards), top_value / len(shards))
        factor_of = factor_of * jnp.repeat(jnp.exp(draws), shape[axis_at] // parts).reshape((-1,) + (1,) * (len(shape) - 1 - axis_at))
    return factor_of


def bell_draw(own_key, shape, width, most, cuts=(), held_as=jnp.bfloat16):
    values = width * jax.random.normal(own_key, shape, jnp.float32)
    if cuts:
        values = values * block_levels(own_key, shape, cuts, -0.22, 0.18)
    return jnp.clip(values, -most, most).astype(held_as)


def setup_inputs(seed: int = 0) -> dict:
    arg_keys = jax.random.split(jax.random.key(seed), 6)
    source_rows = bell_draw(arg_keys[0], (N_DEV * SRC_CAP, FEATS), 1.0, 6.0, ((0, 32),))
    factor = bell_draw(arg_keys[1], (LAYERS, BLOCK, BLOCK), BLOCK ** -0.5, 0.25)
    plan_start = draw_plan_start(jax.random.fold_in(arg_keys[5], 71), 0)
    plan_count = draw_plan_count(jax.random.fold_in(arg_keys[5], 71), 0)
    partners = draw_partners(jax.random.fold_in(arg_keys[5], 71), 0)
    return {"source_rows": source_rows, "factor": factor, "plan_start": plan_start, "plan_count": plan_count, "partners": partners}


def precondition(row_data, factor):
    block_width = factor.shape[1]
    pieces_out = []
    for layer in range(factor.shape[0]):
        pieces_out.append(jnp.dot(row_data[:, layer * block_width:(layer + 1) * block_width], factor[layer], preferred_element_type=jnp.float32))
    return jnp.concatenate(pieces_out, axis=1).astype(jnp.bfloat16)


def balance_index(plan_start, plan_count):
    inclusive = jnp.cumsum(plan_count, axis=0).astype(jnp.int32)
    exclusive = (inclusive - plan_count).astype(jnp.int32)
    positions = jnp.arange(ROWS_DEV, dtype=jnp.int32)

    def one_destination(columns):
        running, earlier, begins = columns
        source_of = jnp.sum((running[None, :] <= positions[:, None]).astype(jnp.int32), axis=1).astype(jnp.int32)
        source_of = jnp.minimum(source_of, N_DEV - 1).astype(jnp.int32)
        return (source_of * SRC_CAP + begins[source_of] + positions - earlier[source_of]).astype(jnp.int32)

    return lax.map(one_destination, (inclusive.T, exclusive.T, plan_start.T))


def reference(source_rows, factor, plan_start, plan_count, partners):
    index_table = balance_index(plan_start, plan_count).reshape(-1).astype(jnp.int32)
    balanced = source_rows[index_table]
    conditioned = precondition(balanced, factor)
    blocks = conditioned.reshape(N_DEV, ROWS_DEV, FEATS)
    scaling = FEATS ** -0.5
    tiles = []
    for round_index in range(ROUNDS):
        pairing = partners[round_index]

        def one_tile(device):
            return jnp.dot(blocks[device], blocks[pairing[device]].T, preferred_element_type=jnp.float32) * scaling

        result = lax.map(one_tile, jnp.arange(N_DEV, dtype=jnp.int32))
        tiles.append(result.reshape(ROWS, ROWS_DEV))
    return jnp.stack(tiles)
```

```python
from functools import partial

import jax
import jax.numpy as jnp
from jax import lax
from jax.experimental import pallas as pl
from jax.experimental.pallas import tpu as pltpu
from jax.sharding import PartitionSpec as P

VMEM_BYTES = 56 * 1024 * 1024


def scatter_kernel(
    dest_ref, place_ref, picked_ref, rows_ref, factor_ref, out_ref, select, stage, sem
):
    layer = pl.program_id(0)
    layers = pl.num_programs(0)
    players, slot_rows, width = stage.shape[1:]
    capacity = rows_ref.shape[0]
    per_part = layers // 4
    part = layer // per_part
    buf = lax.rem(layer, 2)

    @pl.when(layer == 0)
    def _():
        lanes = lax.broadcasted_iota(jnp.int32, select.shape, 1)
        select[...] = (lanes == picked_ref[...]).astype(jnp.float32).astype(jnp.bfloat16)

    conditioned = jnp.dot(
        rows_ref[...], factor_ref[0], preferred_element_type=jnp.float32
    ).astype(jnp.bfloat16)

    def drain(which):
        pltpu.make_async_copy(stage.at[which], stage.at[which], sem.at[which]).wait()

    @pl.when(layer >= 2)
    def _():
        drain(buf)

    moved = jnp.dot(select[...], conditioned, preferred_element_type=jnp.float32)
    stage[buf] = moved.reshape(players, slot_rows, width).astype(jnp.bfloat16)
    column = pl.multiple_of(lax.rem(layer, per_part) * width, width)

    @pl.loop(0, players)
    def _(player):
        at = part * players + player
        pltpu.make_async_copy(
            stage.at[buf, player],
            out_ref.at[dest_ref[at], place_ref[at], :, pl.ds(column, width)],
            sem.at[buf],
        ).start()

    @pl.when(layer == layers - 1)
    def _():
        drain(1 - buf)
        drain(buf)


def tiles_kernel(mate_ref, arrival_ref, received_ref, own_ref, s1_ref, s2_ref, s3_ref, blocks, *, scaling):
    step = pl.program_id(0)
    sources, _, slot_rows, width = received_ref.shape
    rows = arrival_ref.shape[1]
    lanes = lax.broadcasted_iota(jnp.int32, (rows, sources * slot_rows), 1)
    select = (lanes == arrival_ref[0]).astype(jnp.float32).astype(jnp.bfloat16)
    data = received_ref[:, 0]
    if slot_rows % 16:
        data = data.astype(jnp.float32).reshape(sources * slot_rows, width).astype(jnp.bfloat16)
    else:
        data = data.reshape(sources * slot_rows, width)
    blocks[step] = jnp.dot(select, data, preferred_element_type=jnp.float32).astype(jnp.bfloat16)

    def tile(a, b):
        return lax.dot_general(
            blocks[a], blocks[b], (((1,), (1,)), ((), ())), preferred_element_type=jnp.float32
        )

    @pl.when(step == 3)
    def _():
        for r in range(2):
            mate = mate_ref[r]
            own_ref[r] = tile(0, mate) * scaling
            for j, ref in ((1, s1_ref), (2, s2_ref), (3, s3_ref)):
                ref[r] = (tile(j, j ^ mate) * scaling).astype(jnp.bfloat16)


def exchange(low, high, own, s1, s2, s3):
    devices = lax.axis_size("dev")
    total = own
    for value, mask in ((s3, low ^ high), (s1, low), (s2, high)):
        got = lax.ppermute(value, "dev", [(d, d ^ mask) for d in range(devices)])
        total = total + got.astype(jnp.float32)
    return total


def per_device(source_rows, factor, plan_start, plan_count, partners):
    devices = lax.axis_size("dev")
    own_index = lax.axis_index("dev")
    capacity, feat_width = source_rows.shape
    layers, width, _ = factor.shape
    slot_rows = capacity // devices
    block_rows = capacity // 2
    part_width = feat_width // 4
    i32 = jnp.int32

    low = jnp.minimum(partners[0, 0], partners[1, 0])
    high = jnp.maximum(partners[0, 0], partners[1, 0])
    mates = jnp.where(partners[:, 0] == low, 1, 2).astype(i32)

    player = jnp.arange(devices, dtype=i32)[None, :]
    part = jnp.arange(4, dtype=i32)[:, None]
    dest = (player & ~low & ~high) | jnp.where(part & 1, low, 0) | jnp.where(part & 2, high, 0)
    differs = player ^ dest
    place = jnp.where(differs & low, 1, 0) + jnp.where(differs & high, 2, 0)
    dest, place = dest.reshape(-1).astype(i32), place.reshape(-1).astype(i32)

    start_row = lax.dynamic_index_in_dim(plan_start, own_index, 0, keepdims=False)
    count_row = lax.dynamic_index_in_dim(plan_count, own_index, 0, keepdims=False)
    offsets = jnp.arange(slot_rows, dtype=i32)
    usable = offsets[None, :] < count_row[:, None]
    picked = jnp.where(usable, start_row[:, None] + offsets[None, :], -1).reshape(-1, 1)

    send = pl.pallas_call(
        scatter_kernel,
        out_shape=jax.ShapeDtypeStruct((devices, 4, slot_rows, part_width), jnp.bfloat16),
        grid_spec=pltpu.PrefetchScalarGridSpec(
            num_scalar_prefetch=2,
            grid=(layers,),
            in_specs=[
                pl.BlockSpec((capacity, 1), lambda l, *_: (0, 0)),
                pl.BlockSpec((capacity, width), lambda l, *_: (0, l)),
                pl.BlockSpec((1, width, width), lambda l, *_: (l, 0, 0)),
            ],
            out_specs=pl.BlockSpec(memory_space=pl.ANY),
            scratch_shapes=[
                pltpu.VMEM((capacity, capacity), jnp.bfloat16),
                pltpu.VMEM((2, devices, slot_rows, width), jnp.bfloat16),
                pltpu.SemaphoreType.DMA((2,)),
            ],
        ),
        compiler_params=pltpu.CompilerParams(vmem_limit_bytes=VMEM_BYTES),
        name="condition_and_place",
    )(dest, place, picked, source_rows, factor)

    received = lax.all_to_all(send, "dev", split_axis=0, concat_axis=0, tiled=True)

    combos = jnp.stack([jnp.zeros_like(low), low, high, low | high])
    counts = jnp.take(plan_count, own_index ^ combos, axis=1).T
    inclusive = jnp.cumsum(counts, axis=1)
    exclusive = inclusive - counts
    positions = jnp.arange(block_rows, dtype=i32)
    source_of = jnp.sum((inclusive[:, None, :] <= positions[None, :, None]).astype(i32), axis=2)
    source_of = jnp.minimum(source_of, devices - 1)
    one_hot = (source_of[:, :, None] == jnp.arange(devices, dtype=i32)[None, None, :]).astype(i32)
    before = jnp.sum(one_hot * exclusive[:, None, :], axis=2)
    arrival = (source_of * slot_rows + positions[None, :] - before)[:, :, None]

    tile_shape = (2, block_rows, block_rows)
    whole_tile = pl.BlockSpec(tile_shape, lambda j, *_: (0, 0, 0))
    own, s1, s2, s3 = pl.pallas_call(
        partial(tiles_kernel, scaling=feat_width ** (-0.5)),
        out_shape=[jax.ShapeDtypeStruct(tile_shape, jnp.float32)]
        + [jax.ShapeDtypeStruct(tile_shape, jnp.bfloat16)] * 3,
        grid_spec=pltpu.PrefetchScalarGridSpec(
            num_scalar_prefetch=1,
            grid=(4,),
            in_specs=[
                pl.BlockSpec((1, block_rows, 1), lambda j, *_: (j, 0, 0)),
                pl.BlockSpec((devices, 1, slot_rows, part_width), lambda j, *_: (0, j, 0, 0)),
            ],
            out_specs=[whole_tile] * 4,
            scratch_shapes=[pltpu.VMEM((4, block_rows, part_width), jnp.bfloat16)],
        ),
        compiler_params=pltpu.CompilerParams(vmem_limit_bytes=VMEM_BYTES),
        name="compact_and_tiles",
    )(mates, arrival, received)

    levels = devices.bit_length() - 1
    branches, keys = [], []
    for b in range(levels):
        for a in range(b):
            branches.append(partial(exchange, 1 << a, 1 << b))
            keys.append((1 << a) | (1 << b))
    which = jnp.argmax(jnp.asarray(keys, dtype=i32) == (low | high)).astype(i32)
    return lax.switch(which, branches, own, s1, s2, s3)


def solution(mesh):
    placed = (P("dev", None), P(), P(), P(), P())
    return jax.shard_map(
        per_device, mesh=mesh, in_specs=placed, out_specs=P(None, "dev", None), check_vma=False
    )
```

```python
from functools import partial

import jax
import jax.numpy as jnp
from jax import lax
from jax.experimental import pallas as pl
from jax.experimental.pallas import tpu as pltpu
from jax.sharding import PartitionSpec as P

VMEM_BYTES = 56 * 1024 * 1024


def scatter_kernel(
    dest_ref, place_ref, picked_ref, rows_ref, factor_ref, out_ref, select, stage, sem
):
    layer = pl.program_id(0)
    layers = pl.num_programs(0)
    players, slot_rows, width = stage.shape[1:]
    capacity = rows_ref.shape[0]
    per_part = layers // 4
    part = layer // per_part
    buf = lax.rem(layer, 2)

    @pl.when(layer == 0)
    def _():
        lanes = lax.broadcasted_iota(jnp.int32, select.shape, 1)
        select[...] = (lanes == picked_ref[...]).astype(jnp.float32).astype(jnp.bfloat16)

    conditioned = jnp.dot(
        rows_ref[...], factor_ref[0], preferred_element_type=jnp.float32
    ).astype(jnp.bfloat16)

    def drain(which):
        pltpu.make_async_copy(stage.at[which], stage.at[which], sem.at[which]).wait()

    @pl.when(layer >= 2)
    def _():
        drain(buf)

    moved = jnp.dot(select[...], conditioned, preferred_element_type=jnp.float32)
    stage[buf] = moved.reshape(players, slot_rows, width).astype(jnp.bfloat16)
    column = pl.multiple_of(lax.rem(layer, per_part) * width, width)

    @pl.loop(0, players)
    def _(player):
        at = part * players + player
        pltpu.make_async_copy(
            stage.at[buf, player],
            out_ref.at[dest_ref[at], place_ref[at], :, pl.ds(column, width)],
            sem.at[buf],
        ).start()

    @pl.when(layer == layers - 1)
    def _():
        drain(1 - buf)
        drain(buf)


def tiles_kernel(edge_ref, arrival_ref, received_ref, own_ref, s1_ref, s2_ref, s3_ref, blocks, *, scaling):
    step = pl.program_id(0)
    sources, _, slot_rows, width = received_ref.shape
    rows = arrival_ref.shape[1]
    lanes = lax.broadcasted_iota(jnp.int32, (rows, sources * slot_rows), 1)
    select = (lanes == arrival_ref[0]).astype(jnp.float32).astype(jnp.bfloat16)
    data = received_ref[:, 0]
    if slot_rows % 16:
        data = data.astype(jnp.float32).reshape(sources * slot_rows, width).astype(jnp.bfloat16)
    else:
        data = data.reshape(sources * slot_rows, width)
    blocks[step] = jnp.dot(select, data, preferred_element_type=jnp.float32).astype(jnp.bfloat16)

    def tile(a, b):
        return lax.dot_general(
            blocks[a], blocks[b], (((1,), (1,)), ((), ())), preferred_element_type=jnp.float32
        )

    @pl.when(step == 3)
    def _():
        edge = edge_ref[0]
        own_ref[...] = tile(0, edge) * scaling
        s1_ref[...] = (tile(1, 1 ^ (3 - edge)) * scaling).astype(jnp.bfloat16)
        s2_ref[...] = (tile(2, 2 ^ (3 - edge)) * scaling).astype(jnp.bfloat16)
        s3_ref[...] = (tile(3, 3 ^ edge) * scaling).astype(jnp.bfloat16)


def owned_mask(device, low, high):
    return low if bool(device & low) == bool(device & high) else high


def exchange(low, high, own, s1, s2, s3):
    devices = lax.axis_size("dev")
    total = own
    for value, mask in ((s3, low ^ high), (s1, low), (s2, high)):
        got = lax.ppermute(value, "dev", [(d, d ^ mask) for d in range(devices)])
        total = total + got.astype(jnp.float32)
    other = lax.ppermute(
        total.astype(jnp.bfloat16),
        "dev",
        [(d, d ^ owned_mask(d, low, high)) for d in range(devices)],
    )
    return total, other


def per_device(source_rows, factor, plan_start, plan_count, partners):
    devices = lax.axis_size("dev")
    own_index = lax.axis_index("dev")
    capacity, feat_width = source_rows.shape
    layers, width, _ = factor.shape
    slot_rows = capacity // devices
    block_rows = capacity // 2
    part_width = feat_width // 4
    i32 = jnp.int32

    low = jnp.minimum(partners[0, 0], partners[1, 0])
    high = jnp.maximum(partners[0, 0], partners[1, 0])
    mates = jnp.where(partners[:, 0] == low, 1, 2).astype(i32)
    edge = jnp.where(((own_index & low) != 0) == ((own_index & high) != 0), 1, 2).astype(i32)

    player = jnp.arange(devices, dtype=i32)[None, :]
    part = jnp.arange(4, dtype=i32)[:, None]
    dest = (player & ~low & ~high) | jnp.where(part & 1, low, 0) | jnp.where(part & 2, high, 0)
    differs = player ^ dest
    place = jnp.where(differs & low, 1, 0) + jnp.where(differs & high, 2, 0)
    dest, place = dest.reshape(-1).astype(i32), place.reshape(-1).astype(i32)

    start_row = lax.dynamic_index_in_dim(plan_start, own_index, 0, keepdims=False)
    count_row = lax.dynamic_index_in_dim(plan_count, own_index, 0, keepdims=False)
    offsets = jnp.arange(slot_rows, dtype=i32)
    usable = offsets[None, :] < count_row[:, None]
    picked = jnp.where(usable, start_row[:, None] + offsets[None, :], -1).reshape(-1, 1)

    send = pl.pallas_call(
        scatter_kernel,
        out_shape=jax.ShapeDtypeStruct((devices, 4, slot_rows, part_width), jnp.bfloat16),
        grid_spec=pltpu.PrefetchScalarGridSpec(
            num_scalar_prefetch=2,
            grid=(layers,),
            in_specs=[
                pl.BlockSpec((capacity, 1), lambda l, *_: (0, 0)),
                pl.BlockSpec((capacity, width), lambda l, *_: (0, l)),
                pl.BlockSpec((1, width, width), lambda l, *_: (l, 0, 0)),
            ],
            out_specs=pl.BlockSpec(memory_space=pl.ANY),
            scratch_shapes=[
                pltpu.VMEM((capacity, capacity), jnp.bfloat16),
                pltpu.VMEM((2, devices, slot_rows, width), jnp.bfloat16),
                pltpu.SemaphoreType.DMA((2,)),
            ],
        ),
        compiler_params=pltpu.CompilerParams(vmem_limit_bytes=VMEM_BYTES),
        name="condition_and_place",
    )(dest, place, picked, source_rows, factor)

    received = lax.all_to_all(send, "dev", split_axis=0, concat_axis=0, tiled=True)

    combos = jnp.stack([jnp.zeros_like(low), low, high, low | high])
    counts = jnp.take(plan_count, own_index ^ combos, axis=1).T
    inclusive = jnp.cumsum(counts, axis=1)
    exclusive = inclusive - counts
    positions = jnp.arange(block_rows, dtype=i32)
    source_of = jnp.sum((inclusive[:, None, :] <= positions[None, :, None]).astype(i32), axis=2)
    source_of = jnp.minimum(source_of, devices - 1)
    one_hot = (source_of[:, :, None] == jnp.arange(devices, dtype=i32)[None, None, :]).astype(i32)
    before = jnp.sum(one_hot * exclusive[:, None, :], axis=2)
    arrival = (source_of * slot_rows + positions[None, :] - before)[:, :, None]

    tile_shape = (block_rows, block_rows)
    whole_tile = pl.BlockSpec(tile_shape, lambda j, *_: (0, 0))
    own, s1, s2, s3 = pl.pallas_call(
        partial(tiles_kernel, scaling=feat_width ** (-0.5)),
        out_shape=[jax.ShapeDtypeStruct(tile_shape, jnp.float32)]
        + [jax.ShapeDtypeStruct(tile_shape, jnp.bfloat16)] * 3,
        grid_spec=pltpu.PrefetchScalarGridSpec(
            num_scalar_prefetch=1,
            grid=(4,),
            in_specs=[
                pl.BlockSpec((1, block_rows, 1), lambda j, *_: (j, 0, 0)),
                pl.BlockSpec((devices, 1, slot_rows, part_width), lambda j, *_: (0, j, 0, 0)),
            ],
            out_specs=[whole_tile] * 4,
            scratch_shapes=[pltpu.VMEM((4, block_rows, part_width), jnp.bfloat16)],
        ),
        compiler_params=pltpu.CompilerParams(vmem_limit_bytes=VMEM_BYTES),
        name="compact_and_tiles",
    )(edge[None], arrival, received)

    levels = devices.bit_length() - 1
    branches, keys = [], []
    for b in range(levels):
        for a in range(b):
            branches.append(partial(exchange, 1 << a, 1 << b))
            keys.append((1 << a) | (1 << b))
    which = jnp.argmax(jnp.asarray(keys, dtype=i32) == (low | high)).astype(i32)
    total, other = lax.switch(which, branches, own, s1, s2, s3)
    mirrored = other.T.astype(jnp.float32)
    return jnp.where((mates == edge)[:, None, None], total[None], mirrored[None])


def solution(mesh):
    placed = (P("dev", None), P(), P(), P(), P())
    return jax.shard_map(
        per_device, mesh=mesh, in_specs=placed, out_specs=P(None, "dev", None), check_vma=False
    )
```

```python
from functools import partial

import jax
import jax.numpy as jnp
from jax import lax
from jax.experimental import pallas as pl
from jax.experimental.pallas import tpu as pltpu
from jax.sharding import PartitionSpec as P

VMEM_BYTES = 56 * 1024 * 1024


def scatter_kernel(
    dest_ref, place_ref, picked_ref, rows_ref, factor_ref, out_ref, select, stage, sem
):
    part = pl.program_id(0)
    parts = pl.num_programs(0)
    players, slot_rows, width = stage.shape[1:]
    buf = lax.rem(part, 2)

    @pl.when(part == 0)
    def _():
        lanes = lax.broadcasted_iota(jnp.int32, select.shape, 1)
        select[...] = (lanes == picked_ref[...]).astype(jnp.float32).astype(jnp.bfloat16)

    conditioned = jnp.dot(
        rows_ref[...], factor_ref[0], preferred_element_type=jnp.float32
    ).astype(jnp.bfloat16)

    def drain(which):
        pltpu.make_async_copy(stage.at[which], stage.at[which], sem.at[which]).wait()

    @pl.when(part >= 2)
    def _():
        drain(buf)

    moved = jnp.dot(select[...], conditioned, preferred_element_type=jnp.float32)
    stage[buf] = moved.reshape(players, slot_rows, width).astype(jnp.bfloat16)

    @pl.loop(0, players)
    def _(player):
        at = part * players + player
        pltpu.make_async_copy(
            stage.at[buf, player],
            out_ref.at[dest_ref[at], place_ref[at]],
            sem.at[buf],
        ).start()

    @pl.when(part == parts - 1)
    def _():
        drain(1 - buf)
        drain(buf)


def tiles_kernel(edge_ref, arrival_ref, received_ref, *refs, scaling, first, last):
    outs, blocks = refs[:-1], refs[-1]
    if not first:
        sum_ref, outs = outs[0], outs[1:]
    step = pl.program_id(0)
    sources, _, slot_rows, width = received_ref.shape
    rows = arrival_ref.shape[1]
    lanes = lax.broadcasted_iota(jnp.int32, (rows, sources * slot_rows), 1)
    select = (lanes == arrival_ref[0]).astype(jnp.float32).astype(jnp.bfloat16)
    data = received_ref[:, 0]
    if slot_rows % 16:
        data = data.astype(jnp.float32).reshape(sources * slot_rows, width).astype(jnp.bfloat16)
    else:
        data = data.reshape(sources * slot_rows, width)
    blocks[step] = jnp.dot(select, data, preferred_element_type=jnp.float32).astype(jnp.bfloat16)

    def tile(a, b):
        return lax.dot_general(
            blocks[a], blocks[b], (((1,), (1,)), ((), ())), preferred_element_type=jnp.float32
        )

    @pl.when(step == 3)
    def _():
        edge = edge_ref[0]
        mates = (edge, 1 ^ (3 - edge), 2 ^ (3 - edge), 3 ^ edge)
        for player, mate in enumerate(mates):
            total = tile(player, mate)
            if not first:
                total = total + sum_ref[player]
            if last:
                outs[player][...] = (total * scaling).astype(outs[player].dtype)
            else:
                outs[0][player] = total


def owned_mask(device, low, high):
    return low if bool(device & low) == bool(device & high) else high


def exchange(low, high, own, s1, s2, s3):
    devices = lax.axis_size("dev")
    total = own
    for value, mask in ((s3, low ^ high), (s1, low), (s2, high)):
        got = lax.ppermute(value, "dev", [(d, d ^ mask) for d in range(devices)])
        total = total + got.astype(jnp.float32)
    other = lax.ppermute(
        total.astype(jnp.bfloat16),
        "dev",
        [(d, d ^ owned_mask(d, low, high)) for d in range(devices)],
    )
    return total, other


def per_device(source_rows, factor, plan_start, plan_count, partners):
    devices = lax.axis_size("dev")
    own_index = lax.axis_index("dev")
    capacity, feat_width = source_rows.shape
    layers, width, _ = factor.shape
    slot_rows = capacity // devices
    block_rows = capacity // 2
    per_part = layers // 4
    i32 = jnp.int32

    low = jnp.minimum(partners[0, 0], partners[1, 0])
    high = jnp.maximum(partners[0, 0], partners[1, 0])
    mates = jnp.where(partners[:, 0] == low, 1, 2).astype(i32)
    edge = jnp.where(((own_index & low) != 0) == ((own_index & high) != 0), 1, 2).astype(i32)

    player = jnp.arange(devices, dtype=i32)[None, :]
    part = jnp.arange(4, dtype=i32)[:, None]
    dest = (player & ~low & ~high) | jnp.where(part & 1, low, 0) | jnp.where(part & 2, high, 0)
    differs = player ^ dest
    place = jnp.where(differs & low, 1, 0) + jnp.where(differs & high, 2, 0)
    dest, place = dest.reshape(-1).astype(i32), place.reshape(-1).astype(i32)

    start_row = lax.dynamic_index_in_dim(plan_start, own_index, 0, keepdims=False)
    count_row = lax.dynamic_index_in_dim(plan_count, own_index, 0, keepdims=False)
    offsets = jnp.arange(slot_rows, dtype=i32)
    usable = offsets[None, :] < count_row[:, None]
    picked = jnp.where(usable, start_row[:, None] + offsets[None, :], -1).reshape(-1, 1)

    sent = []
    for chunk in range(per_part):
        layer_of = partial(lambda chunk, p: p * per_part + chunk, chunk)
        sent.append(pl.pallas_call(
            scatter_kernel,
            out_shape=jax.ShapeDtypeStruct((devices, 4, slot_rows, width), jnp.bfloat16),
            grid_spec=pltpu.PrefetchScalarGridSpec(
                num_scalar_prefetch=2,
                grid=(4,),
                in_specs=[
                    pl.BlockSpec((capacity, 1), lambda p, *_: (0, 0)),
                    pl.BlockSpec((capacity, width), lambda p, *_, f=layer_of: (0, f(p))),
                    pl.BlockSpec((1, width, width), lambda p, *_, f=layer_of: (f(p), 0, 0)),
                ],
                out_specs=pl.BlockSpec(memory_space=pl.ANY),
                scratch_shapes=[
                    pltpu.VMEM((capacity, capacity), jnp.bfloat16),
                    pltpu.VMEM((2, devices, slot_rows, width), jnp.bfloat16),
                    pltpu.SemaphoreType.DMA((2,)),
                ],
            ),
            compiler_params=pltpu.CompilerParams(vmem_limit_bytes=VMEM_BYTES),
            cost_estimate=pl.CostEstimate(
                flops=8 * capacity * width * (width + capacity),
                bytes_accessed=16 * capacity * width + 8 * width * width,
                transcendentals=0,
            ),
            name=f"condition_and_place_{chunk}",
        )(dest, place, picked, source_rows, factor))

    received = [
        lax.all_to_all(send, "dev", split_axis=0, concat_axis=0, tiled=True) for send in sent
    ]

    combos = jnp.stack([jnp.zeros_like(low), low, high, low | high])
    counts = jnp.take(plan_count, own_index ^ combos, axis=1).T
    inclusive = jnp.cumsum(counts, axis=1)
    exclusive = inclusive - counts
    positions = jnp.arange(block_rows, dtype=i32)
    source_of = jnp.sum((inclusive[:, None, :] <= positions[None, :, None]).astype(i32), axis=2)
    source_of = jnp.minimum(source_of, devices - 1)
    one_hot = (source_of[:, :, None] == jnp.arange(devices, dtype=i32)[None, None, :]).astype(i32)
    before = jnp.sum(one_hot * exclusive[:, None, :], axis=2)
    arrival = (source_of * slot_rows + positions[None, :] - before)[:, :, None]

    tile_shape = (block_rows, block_rows)
    whole_tile = pl.BlockSpec(tile_shape, lambda j, *_: (0, 0))
    sums_shape = jax.ShapeDtypeStruct((4,) + tile_shape, jnp.float32)
    sums_spec = pl.BlockSpec((4,) + tile_shape, lambda j, *_: (0, 0, 0))
    sums = []
    for chunk in range(per_part):
        last = chunk == per_part - 1
        out_shape, out_specs = [sums_shape], [sums_spec]
        if last:
            out_shape = [jax.ShapeDtypeStruct(tile_shape, jnp.float32)]
            out_shape += [jax.ShapeDtypeStruct(tile_shape, jnp.bfloat16)] * 3
            out_specs = [whole_tile] * 4
        sums = pl.pallas_call(
            partial(tiles_kernel, scaling=feat_width ** (-0.5), first=chunk == 0, last=last),
            out_shape=out_shape,
            grid_spec=pltpu.PrefetchScalarGridSpec(
                num_scalar_prefetch=1,
                grid=(4,),
                in_specs=[
                    pl.BlockSpec((1, block_rows, 1), lambda j, *_: (j, 0, 0)),
                    pl.BlockSpec((devices, 1, slot_rows, width), lambda j, *_: (0, j, 0, 0)),
                ] + [sums_spec] * len(sums),
                out_specs=out_specs,
                scratch_shapes=[pltpu.VMEM((4, block_rows, width), jnp.bfloat16)],
            ),
            compiler_params=pltpu.CompilerParams(vmem_limit_bytes=VMEM_BYTES),
            cost_estimate=pl.CostEstimate(
                flops=8 * block_rows * width * (capacity + block_rows),
                bytes_accessed=8 * capacity * width + 16 * block_rows * block_rows,
                transcendentals=0,
            ),
            name=f"compact_and_tiles_{chunk}",
        )(edge[None], arrival, received[chunk], *sums)
    own, s1, s2, s3 = sums

    levels = devices.bit_length() - 1
    branches, keys = [], []
    for b in range(levels):
        for a in range(b):
            branches.append(partial(exchange, 1 << a, 1 << b))
            keys.append((1 << a) | (1 << b))
    which = jnp.argmax(jnp.asarray(keys, dtype=i32) == (low | high)).astype(i32)
    total, other = lax.switch(which, branches, own, s1, s2, s3)
    mirrored = other.T.astype(jnp.float32)
    return jnp.where((mates == edge)[:, None, None], total[None], mirrored[None])


def solution(mesh):
    placed = (P("dev", None), P(), P(), P(), P())
    return jax.shard_map(
        per_device, mesh=mesh, in_specs=placed, out_specs=P(None, "dev", None), check_vma=False
    )
```

```python
from functools import partial

import jax
import jax.numpy as jnp
from jax import lax
from jax.experimental import pallas as pl
from jax.experimental.pallas import tpu as pltpu
from jax.sharding import PartitionSpec as P

VMEM_BYTES = 56 * 1024 * 1024


def scatter_kernel(
    own_ref, partners_ref, start_ref, count_ref, rows_ref, factor_ref, out_ref, picked, select, stage, sem
):
    part = pl.program_id(0)
    parts = pl.num_programs(0)
    players, slot_rows, width = stage.shape[1:]
    buf = lax.rem(part, 2)

    @pl.when(part == 0)
    def _():
        offsets = lax.broadcasted_iota(jnp.int32, (slot_rows, picked.shape[1]), 0)

        @pl.loop(0, players)
        def _(player):
            start, count = start_ref[own_ref[0], player], count_ref[own_ref[0], player]
            slot = pl.ds(pl.multiple_of(player * slot_rows, slot_rows), slot_rows)
            picked[slot, :] = jnp.where(offsets < count, start + offsets, -1)

        lanes = lax.broadcasted_iota(jnp.int32, select.shape, 1)
        select[...] = (lanes == picked[:, :1]).astype(jnp.float32).astype(jnp.bfloat16)

    conditioned = jnp.dot(
        rows_ref[...], factor_ref[0], preferred_element_type=jnp.float32
    ).astype(jnp.bfloat16)

    def drain(which):
        pltpu.make_async_copy(stage.at[which], stage.at[which], sem.at[which]).wait()

    @pl.when(part >= 2)
    def _():
        drain(buf)

    moved = jnp.dot(select[...], conditioned, preferred_element_type=jnp.float32)
    stage[buf] = moved.reshape(players, slot_rows, width).astype(jnp.bfloat16)

    low = jnp.minimum(partners_ref[0, 0], partners_ref[1, 0])
    high = jnp.maximum(partners_ref[0, 0], partners_ref[1, 0])
    bits = jnp.where((part & 1) != 0, low, 0) | jnp.where((part & 2) != 0, high, 0)

    @pl.loop(0, players)
    def _(player):
        dest = (player & ~(low | high)) | bits
        differs = player ^ dest
        place = jnp.where((differs & low) != 0, 1, 0) + jnp.where((differs & high) != 0, 2, 0)
        pltpu.make_async_copy(
            stage.at[buf, player],
            out_ref.at[dest, place],
            sem.at[buf],
        ).start()

    @pl.when(part == parts - 1)
    def _():
        drain(1 - buf)
        drain(buf)


def tiles_kernel(edge_ref, arrival_ref, received_ref, *refs, scaling, first, last):
    outs, blocks = refs[:-1], refs[-1]
    if not first:
        sum_ref, outs = outs[0], outs[1:]
    step = pl.program_id(0)
    sources, _, slot_rows, width = received_ref.shape
    rows = arrival_ref.shape[1]
    lanes = lax.broadcasted_iota(jnp.int32, (rows, sources * slot_rows), 1)
    select = (lanes == arrival_ref[0]).astype(jnp.float32).astype(jnp.bfloat16)
    data = received_ref[:, 0]
    if slot_rows % 16:
        data = data.astype(jnp.float32).reshape(sources * slot_rows, width).astype(jnp.bfloat16)
    else:
        data = data.reshape(sources * slot_rows, width)
    blocks[step] = jnp.dot(select, data, preferred_element_type=jnp.float32).astype(jnp.bfloat16)

    def tile(a, b):
        return lax.dot_general(
            blocks[a], blocks[b], (((1,), (1,)), ((), ())), preferred_element_type=jnp.float32
        )

    @pl.when(step == 3)
    def _():
        edge = edge_ref[0]
        mates = (edge, 1 ^ (3 - edge), 2 ^ (3 - edge), 3 ^ edge)
        for player, mate in enumerate(mates):
            total = tile(player, mate)
            if not first:
                total = total + sum_ref[player]
            if last:
                outs[player][...] = (total * scaling).astype(outs[player].dtype)
            else:
                outs[0][player] = total


def owned_mask(device, low, high):
    return low if bool(device & low) == bool(device & high) else high


def exchange(low, high, own, s1, s2, s3):
    devices = lax.axis_size("dev")
    total = own
    for value, mask in ((s3, low ^ high), (s1, low), (s2, high)):
        got = lax.ppermute(value, "dev", [(d, d ^ mask) for d in range(devices)])
        total = total + got.astype(jnp.float32)
    other = lax.ppermute(
        total.astype(jnp.bfloat16),
        "dev",
        [(d, d ^ owned_mask(d, low, high)) for d in range(devices)],
    )
    return total, other


def per_device(source_rows, factor, plan_start, plan_count, partners):
    devices = lax.axis_size("dev")
    own_index = lax.axis_index("dev")
    capacity, feat_width = source_rows.shape
    layers, width, _ = factor.shape
    slot_rows = capacity // devices
    block_rows = capacity // 2
    per_part = layers // 4
    i32 = jnp.int32

    low = jnp.minimum(partners[0, 0], partners[1, 0])
    high = jnp.maximum(partners[0, 0], partners[1, 0])
    mates = jnp.where(partners[:, 0] == low, 1, 2).astype(i32)
    edge = jnp.where(((own_index & low) != 0) == ((own_index & high) != 0), 1, 2).astype(i32)

    sent = []
    for chunk in range(per_part):
        layer_of = partial(lambda chunk, p: p * per_part + chunk, chunk)
        sent.append(pl.pallas_call(
            scatter_kernel,
            out_shape=jax.ShapeDtypeStruct((devices, 4, slot_rows, width), jnp.bfloat16),
            grid_spec=pltpu.PrefetchScalarGridSpec(
                num_scalar_prefetch=4,
                grid=(4,),
                in_specs=[
                    pl.BlockSpec((capacity, width), lambda p, *_, f=layer_of: (0, f(p))),
                    pl.BlockSpec((1, width, width), lambda p, *_, f=layer_of: (f(p), 0, 0)),
                ],
                out_specs=pl.BlockSpec(memory_space=pl.ANY),
                scratch_shapes=[
                    pltpu.VMEM((capacity, 128), jnp.int32),
                    pltpu.VMEM((capacity, capacity), jnp.bfloat16),
                    pltpu.VMEM((2, devices, slot_rows, width), jnp.bfloat16),
                    pltpu.SemaphoreType.DMA((2,)),
                ],
            ),
            compiler_params=pltpu.CompilerParams(vmem_limit_bytes=VMEM_BYTES),
            cost_estimate=pl.CostEstimate(
                flops=8 * capacity * width * (width + capacity),
                bytes_accessed=16 * capacity * width + 8 * width * width,
                transcendentals=0,
            ),
            name=f"condition_and_place_{chunk}",
        )(own_index[None], partners, plan_start, plan_count, source_rows, factor))

    received = [
        lax.all_to_all(send, "dev", split_axis=0, concat_axis=0, tiled=True) for send in sent
    ]

    combos = jnp.stack([jnp.zeros_like(low), low, high, low | high])
    counts = jnp.take(plan_count, own_index ^ combos, axis=1).T
    inclusive = jnp.cumsum(counts, axis=1)
    exclusive = inclusive - counts
    positions = jnp.arange(block_rows, dtype=i32)
    source_of = jnp.sum((inclusive[:, None, :] <= positions[None, :, None]).astype(i32), axis=2)
    source_of = jnp.minimum(source_of, devices - 1)
    one_hot = (source_of[:, :, None] == jnp.arange(devices, dtype=i32)[None, None, :]).astype(i32)
    before = jnp.sum(one_hot * exclusive[:, None, :], axis=2)
    arrival = (source_of * slot_rows + positions[None, :] - before)[:, :, None]

    tile_shape = (block_rows, block_rows)
    whole_tile = pl.BlockSpec(tile_shape, lambda j, *_: (0, 0))
    sums_shape = jax.ShapeDtypeStruct((4,) + tile_shape, jnp.float32)
    sums_spec = pl.BlockSpec((4,) + tile_shape, lambda j, *_: (0, 0, 0))
    sums = []
    for chunk in range(per_part):
        last = chunk == per_part - 1
        out_shape, out_specs = [sums_shape], [sums_spec]
        if last:
            out_shape = [jax.ShapeDtypeStruct(tile_shape, jnp.float32)]
            out_shape += [jax.ShapeDtypeStruct(tile_shape, jnp.bfloat16)] * 3
            out_specs = [whole_tile] * 4
        sums = pl.pallas_call(
            partial(tiles_kernel, scaling=feat_width ** (-0.5), first=chunk == 0, last=last),
            out_shape=out_shape,
            grid_spec=pltpu.PrefetchScalarGridSpec(
                num_scalar_prefetch=1,
                grid=(4,),
                in_specs=[
                    pl.BlockSpec((1, block_rows, 1), lambda j, *_: (j, 0, 0)),
                    pl.BlockSpec((devices, 1, slot_rows, width), lambda j, *_: (0, j, 0, 0)),
                ] + [sums_spec] * len(sums),
                out_specs=out_specs,
                scratch_shapes=[pltpu.VMEM((4, block_rows, width), jnp.bfloat16)],
            ),
            compiler_params=pltpu.CompilerParams(vmem_limit_bytes=VMEM_BYTES),
            cost_estimate=pl.CostEstimate(
                flops=8 * block_rows * width * (capacity + block_rows),
                bytes_accessed=8 * capacity * width + 16 * block_rows * block_rows,
                transcendentals=0,
            ),
            name=f"compact_and_tiles_{chunk}",
        )(edge[None], arrival, received[chunk], *sums)
    own, s1, s2, s3 = sums

    levels = devices.bit_length() - 1
    branches, keys = [], []
    for b in range(levels):
        for a in range(b):
            branches.append(partial(exchange, 1 << a, 1 << b))
            keys.append((1 << a) | (1 << b))
    which = jnp.argmax(jnp.asarray(keys, dtype=i32) == (low | high)).astype(i32)
    total, other = lax.switch(which, branches, own, s1, s2, s3)
    mirrored = other.T.astype(jnp.float32)
    return jnp.where((mates == edge)[:, None, None], total[None], mirrored[None])


def solution(mesh):
    placed = (P("dev", None), P(), P(), P(), P())
    return jax.shard_map(
        per_device, mesh=mesh, in_specs=placed, out_specs=P(None, "dev", None), check_vma=False
    )
```

```python
from functools import partial

import jax
import jax.numpy as jnp
from jax import lax
from jax.experimental import pallas as pl
from jax.experimental.pallas import tpu as pltpu
from jax.sharding import PartitionSpec as P

VMEM_BYTES = 56 * 1024 * 1024


def scatter_kernel(
    own_ref, partners_ref, start_ref, count_ref, rows_ref, factor_ref, out_ref, picked, select, stage, sem
):
    part = pl.program_id(0)
    parts = pl.num_programs(0)
    players, slot_rows, width = stage.shape[1:]
    buf = lax.rem(part, 2)

    @pl.when(part == 0)
    def _():
        offsets = lax.broadcasted_iota(jnp.int32, (slot_rows, picked.shape[1]), 0)

        @pl.loop(0, players)
        def _(player):
            start, count = start_ref[own_ref[0], player], count_ref[own_ref[0], player]
            slot = pl.ds(pl.multiple_of(player * slot_rows, slot_rows), slot_rows)
            picked[slot, :] = jnp.where(offsets < count, start + offsets, -1)

        lanes = lax.broadcasted_iota(jnp.int32, select.shape, 1)
        select[...] = (lanes == picked[:, :1]).astype(jnp.float32).astype(jnp.bfloat16)

    conditioned = jnp.dot(
        rows_ref[...], factor_ref[0], preferred_element_type=jnp.float32
    ).astype(jnp.bfloat16)

    def drain(which):
        pltpu.make_async_copy(stage.at[which], stage.at[which], sem.at[which]).wait()

    @pl.when(part >= 2)
    def _():
        drain(buf)

    moved = jnp.dot(select[...], conditioned, preferred_element_type=jnp.float32)
    stage[buf] = moved.reshape(players, slot_rows, width).astype(jnp.bfloat16)

    low = jnp.minimum(partners_ref[0, 0], partners_ref[1, 0])
    high = jnp.maximum(partners_ref[0, 0], partners_ref[1, 0])
    bits = jnp.where((part & 1) != 0, low, 0) | jnp.where((part & 2) != 0, high, 0)

    @pl.loop(0, players)
    def _(player):
        dest = (player & ~(low | high)) | bits
        differs = player ^ dest
        place = jnp.where((differs & low) != 0, 1, 0) + jnp.where((differs & high) != 0, 2, 0)
        pltpu.make_async_copy(
            stage.at[buf, player],
            out_ref.at[dest, place],
            sem.at[buf],
        ).start()

    @pl.when(part == parts - 1)
    def _():
        drain(1 - buf)
        drain(buf)


def tiles_kernel(edge_ref, arrival_ref, received_ref, *refs, scaling, first, last):
    outs, blocks = refs[:-1], refs[-1]
    if not first:
        sum_ref, outs = outs[0], outs[1:]
    step = pl.program_id(0)
    sources, _, slot_rows, width = received_ref.shape
    rows = arrival_ref.shape[1]
    lanes = lax.broadcasted_iota(jnp.int32, (rows, sources * slot_rows), 1)
    select = (lanes == arrival_ref[0]).astype(jnp.float32).astype(jnp.bfloat16)
    data = received_ref[:, 0]
    if slot_rows % 16:
        data = data.astype(jnp.float32).reshape(sources * slot_rows, width).astype(jnp.bfloat16)
    else:
        data = data.reshape(sources * slot_rows, width)
    blocks[step] = jnp.dot(select, data, preferred_element_type=jnp.float32).astype(jnp.bfloat16)

    def tile(a, b):
        return lax.dot_general(
            blocks[a], blocks[b], (((1,), (1,)), ((), ())), preferred_element_type=jnp.float32
        )

    @pl.when(step == 3)
    def _():
        edge = edge_ref[0]
        mates = (edge, 1 ^ (3 - edge), 2 ^ (3 - edge), 3 ^ edge)
        for player, mate in enumerate(mates):
            total = tile(player, mate)
            if not first:
                total = total + sum_ref[player]
            if last:
                outs[player][...] = (total * scaling).astype(outs[player].dtype)
            else:
                outs[0][player] = total


def owned_mask(device, low, high):
    return low if bool(device & low) == bool(device & high) else high


def exchange(low, high, own, s1, s2, s3):
    devices = lax.axis_size("dev")

    def across(value, mask):
        got = lax.ppermute(value, "dev", [(d, d ^ mask) for d in range(devices)])
        return got.astype(jnp.float32)

    if low == 1:
        pair = s2.astype(jnp.float32) + across(s3, low)
        total = own + across(s1, low)
        total = total + across(pair.astype(jnp.bfloat16), high)
    else:
        total = own + across(s3, low ^ high) + across(s1, low) + across(s2, high)
    other = lax.ppermute(
        total.astype(jnp.bfloat16),
        "dev",
        [(d, d ^ owned_mask(d, low, high)) for d in range(devices)],
    )
    return total, other


def per_device(source_rows, factor, plan_start, plan_count, partners):
    devices = lax.axis_size("dev")
    own_index = lax.axis_index("dev")
    capacity, feat_width = source_rows.shape
    layers, width, _ = factor.shape
    slot_rows = capacity // devices
    block_rows = capacity // 2
    per_part = layers // 4
    i32 = jnp.int32

    low = jnp.minimum(partners[0, 0], partners[1, 0])
    high = jnp.maximum(partners[0, 0], partners[1, 0])
    mates = jnp.where(partners[:, 0] == low, 1, 2).astype(i32)
    edge = jnp.where(((own_index & low) != 0) == ((own_index & high) != 0), 1, 2).astype(i32)

    sent = []
    for chunk in range(per_part):
        layer_of = partial(lambda chunk, p: p * per_part + chunk, chunk)
        sent.append(pl.pallas_call(
            scatter_kernel,
            out_shape=jax.ShapeDtypeStruct((devices, 4, slot_rows, width), jnp.bfloat16),
            grid_spec=pltpu.PrefetchScalarGridSpec(
                num_scalar_prefetch=4,
                grid=(4,),
                in_specs=[
                    pl.BlockSpec((capacity, width), lambda p, *_, f=layer_of: (0, f(p))),
                    pl.BlockSpec((1, width, width), lambda p, *_, f=layer_of: (f(p), 0, 0)),
                ],
                out_specs=pl.BlockSpec(memory_space=pl.ANY),
                scratch_shapes=[
                    pltpu.VMEM((capacity, 128), jnp.int32),
                    pltpu.VMEM((capacity, capacity), jnp.bfloat16),
                    pltpu.VMEM((2, devices, slot_rows, width), jnp.bfloat16),
                    pltpu.SemaphoreType.DMA((2,)),
                ],
            ),
            compiler_params=pltpu.CompilerParams(vmem_limit_bytes=VMEM_BYTES),
            cost_estimate=pl.CostEstimate(
                flops=8 * capacity * width * (width + capacity),
                bytes_accessed=16 * capacity * width + 8 * width * width,
                transcendentals=0,
            ),
            name=f"condition_and_place_{chunk}",
        )(own_index[None], partners, plan_start, plan_count, source_rows, factor))

    received = [
        lax.all_to_all(send, "dev", split_axis=0, concat_axis=0, tiled=True) for send in sent
    ]

    combos = jnp.stack([jnp.zeros_like(low), low, high, low | high])
    counts = jnp.take(plan_count, own_index ^ combos, axis=1).T
    inclusive = jnp.cumsum(counts, axis=1)
    exclusive = inclusive - counts
    positions = jnp.arange(block_rows, dtype=i32)
    source_of = jnp.sum((inclusive[:, None, :] <= positions[None, :, None]).astype(i32), axis=2)
    source_of = jnp.minimum(source_of, devices - 1)
    one_hot = (source_of[:, :, None] == jnp.arange(devices, dtype=i32)[None, None, :]).astype(i32)
    before = jnp.sum(one_hot * exclusive[:, None, :], axis=2)
    arrival = (source_of * slot_rows + positions[None, :] - before)[:, :, None]

    tile_shape = (block_rows, block_rows)
    whole_tile = pl.BlockSpec(tile_shape, lambda j, *_: (0, 0))
    sums_shape = jax.ShapeDtypeStruct((4,) + tile_shape, jnp.float32)
    sums_spec = pl.BlockSpec((4,) + tile_shape, lambda j, *_: (0, 0, 0))
    sums = []
    for chunk in range(per_part):
        last = chunk == per_part - 1
        out_shape, out_specs = [sums_shape], [sums_spec]
        if last:
            out_shape = [jax.ShapeDtypeStruct(tile_shape, jnp.float32)]
            out_shape += [jax.ShapeDtypeStruct(tile_shape, jnp.bfloat16)] * 3
            out_specs = [whole_tile] * 4
        sums = pl.pallas_call(
            partial(tiles_kernel, scaling=feat_width ** (-0.5), first=chunk == 0, last=last),
            out_shape=out_shape,
            grid_spec=pltpu.PrefetchScalarGridSpec(
                num_scalar_prefetch=1,
                grid=(4,),
                in_specs=[
                    pl.BlockSpec((1, block_rows, 1), lambda j, *_: (j, 0, 0)),
                    pl.BlockSpec((devices, 1, slot_rows, width), lambda j, *_: (0, j, 0, 0)),
                ] + [sums_spec] * len(sums),
                out_specs=out_specs,
                scratch_shapes=[pltpu.VMEM((4, block_rows, width), jnp.bfloat16)],
            ),
            compiler_params=pltpu.CompilerParams(vmem_limit_bytes=VMEM_BYTES),
            cost_estimate=pl.CostEstimate(
                flops=8 * block_rows * width * (capacity + block_rows),
                bytes_accessed=8 * capacity * width + 16 * block_rows * block_rows,
                transcendentals=0,
            ),
            name=f"compact_and_tiles_{chunk}",
        )(edge[None], arrival, received[chunk], *sums)
    own, s1, s2, s3 = sums

    levels = devices.bit_length() - 1
    branches, keys = [], []
    for b in range(levels):
        for a in range(b):
            branches.append(partial(exchange, 1 << a, 1 << b))
            keys.append((1 << a) | (1 << b))
    which = jnp.argmax(jnp.asarray(keys, dtype=i32) == (low | high)).astype(i32)
    total, other = lax.switch(which, branches, own, s1, s2, s3)
    mirrored = other.T.astype(jnp.float32)
    return jnp.where((mates == edge)[:, None, None], total[None], mirrored[None])


def solution(mesh):
    placed = (P("dev", None), P(), P(), P(), P())
    return jax.shard_map(
        per_device, mesh=mesh, in_specs=placed, out_specs=P(None, "dev", None), check_vma=False
    )
```
